32 devices in a mesh: groups: 2 (over y), seq: 16 (over z, x, core).
Axes of the slice: x: 2, y: 2, z: 4, core: 2. Of those that a mesh axis runs over, the one named last changes fastest.
Arguments:
- queries: bfloat16 [8192, 2048], P(('groups', 'seq')), parts along dimension 0
- keys: bfloat16 [8192, 2048], P(('groups', 'seq')), parts along dimension 0
- values: bfloat16 [8192, 2048], P(('groups', 'seq')), parts along dimension 0, may hold values from -6 to 6
- grad_out: bfloat16 [8192, 2048], P(('groups', 'seq')), parts along dimension 0, may hold values from -15 to 15
- global_blocks: int32 [4], P('groups'), parts along dimension 0, may hold values from 0 to 63, as said below
- random_blocks: int32 [32, 64, 3], P('groups'), parts along dimension 0, may hold values from 0 to 63, as said below
Outputs:
- attended: bfloat16 [8192, 2048], P(('groups', 'seq')), parts along dimension 0
- grad_q: bfloat16 [8192, 2048], P(('groups', 'seq')), parts along dimension 0
- grad_k: bfloat16 [8192, 2048], P(('groups', 'seq')), parts along dimension 0
- grad_v: bfloat16 [8192, 2048], P(('groups', 'seq')), parts along dimension 0
The draws below stay inside these ranges and needn't reach their ends.
There are 2 independent parts, one for each index of `groups`. The reference program is written for one: setup_inputs(seed, part) draws one part's arguments, and reference() takes and returns one part's arrays. A program takes and returns all parts, laid end to end along the dimension named above; each array names one. Nothing has to cross between parts.
Inputs may be any that keep to these rules, and one draw needn't show every extreme that they name: `global_blocks`: the 2 entries are distinct blocks. `random_blocks`: among the 192 entries for the query blocks of one index s of seq (blocks s * 4 to s * 4 + 3, all heads and slots), at most 12 name blocks of any one index of seq, and in every draw some index is named exactly 12 times by some index.
All inputs are finite; a program needn't handle non-finite values.
Results may differ from the reference program's by a relative error of at most 0.0057.
Values may be sent and summed in bfloat16 or wider, within the bound.
A program may use at most 192 MiB of HBM per device.

```python
import math
import jax
import jax.numpy as jnp
from jax import lax

HEADS = 16
HEAD_DIM = 128
BLOCK = 64
GLOBALS = 2
RANDOM = 3
DEV_BLOCKS = 4
WIDTH = 2048
BLOCKS = 64
LENGTH = 4096
REQUESTS = 192
CAPACITY = 12


def draw_queries(key, part):
    key = jax.random.fold_in(key, 1)
    field = jnp.clip(1.4 * jax.random.normal(key, (LENGTH, WIDTH), jnp.float32), -6.0, 6.0)
    return field.astype(jnp.bfloat16)


def draw_keys(key, part):
    key = jax.random.fold_in(key, 4)
    field = jnp.clip(1.4 * jax.random.normal(key, (LENGTH, WIDTH), jnp.float32), -6.0, 6.0)
    return field.astype(jnp.bfloat16)


def draw_global_blocks(key, part):
    key = jax.random.fold_in(key, 2)
    return jax.random.permutation(key, BLOCKS)[:GLOBALS].astype(jnp.int32)


def draw_random_blocks(key, part):
    key = jax.random.fold_in(key, 3)
    shards = BLOCKS // DEV_BLOCKS

    def one_device(device_key):
        rounds_list = [jax.random.permutation(jax.random.fold_in(device_key, turn), shards) for turn in range(CAPACITY)]
        owners = jnp.concatenate(rounds_list)[:REQUESTS]
        owners = jax.random.permutation(jax.random.fold_in(device_key, 999), owners)
        within = jax.random.randint(jax.random.fold_in(device_key, 1000), (REQUESTS,), 0, DEV_BLOCKS)
        return (owners * DEV_BLOCKS + within).astype(jnp.int32)
    device_keys = jax.random.split(key, shards)
    request_table = jax.vmap(one_device)(device_keys)
    request_table = request_table.reshape(shards, HEADS, DEV_BLOCKS, RANDOM)
    return jnp.transpose(request_table, (1, 0, 2, 3)).reshape(HEADS, BLOCKS, RANDOM).astype(jnp.int32)


def block_levels(own_key, shape, cuts, smallest, largest):
    def one(axis_at, parts):
        heights = jax.random.uniform(jax.random.fold_in(jax.random.fold_in(own_key, 6), axis_at), (parts,), jnp.float32, smallest / len(cuts), largest / len(cuts))
        return jnp.repeat(jnp.exp(heights), shape[axis_at] // parts).reshape((-1,) + (1,) * (len(shape) - axis_at - 1))

    level = one(*cuts[0])
    for cut in cuts[1:]:
        level = level * one(*cut)
    return level


def normal_values(key, dims, width, limit, cuts=(), kind=jnp.bfloat16):
    drawn = width * jax.random.normal(key, dims, jnp.float32)
    if cuts:
        drawn = drawn * block_levels(key, dims, cuts, -0.22, 0.18)
    return jnp.clip(drawn, -limit, limit).astype(kind)


def setup_inputs(seed: int = 0, part: int = 0) -> dict:
    key_of = jax.random.split(jax.random.key(seed), 7)
    part_splits = jax.random.split(jax.random.fold_in(key_of[6], part), 7)
    queries = draw_queries(jax.random.fold_in(jax.random.fold_in(key_of[6], part), 71), part)
    keys = draw_keys(jax.random.fold_in(jax.random.fold_in(key_of[6], part), 71), part)
    values = normal_values(part_splits[2], (LENGTH, WIDTH), 1.0, 6.0, ((0, 16),))
    grad_out = normal_values(part_splits[3], (LENGTH, WIDTH), 3.0, 15.0, ((0, 16),))
    global_blocks = draw_global_blocks(jax.random.fold_in(jax.random.fold_in(key_of[6], part), 71), part)
    random_blocks = draw_random_blocks(jax.random.fold_in(jax.random.fold_in(key_of[6], part), 71), part)
    return dict(queries=queries, keys=keys, values=values, grad_out=grad_out, global_blocks=global_blocks, random_blocks=random_blocks)


MASKED = -1e+30

def rounded(value):
    return lax.optimization_barrier(value.astype(jnp.bfloat16)).astype(jnp.float32)

def reference(queries, keys, values, grad_out, global_blocks, random_blocks):
    score_scale = 1.0 / math.sqrt(HEAD_DIM)
    block_shape = (BLOCKS, BLOCK, HEADS, HEAD_DIM)
    q_all = queries.reshape(block_shape)
    k_all = keys.reshape(block_shape)
    v_all = values.reshape(block_shape)
    d_all = grad_out.reshape(block_shape)
    head_index = jnp.arange(HEADS, dtype=jnp.int32)[:, None]
    k_glob = k_all[global_blocks].astype(jnp.float32)
    v_glob = v_all[global_blocks].astype(jnp.float32)
    n_near = 3 * BLOCK
    n_glob = GLOBALS * BLOCK

    def split_keys(value):
        near_part = value[..., :n_near].reshape(HEADS, BLOCK, 3, BLOCK)
        glob_part = value[..., n_near:n_near + n_glob].reshape(HEADS, BLOCK, GLOBALS, BLOCK)
        rand_part = value[..., n_near + n_glob:].reshape(HEADS, BLOCK, RANDOM, BLOCK)
        return (near_part, glob_part, rand_part)

    def visit_block(carry, block_id):
        acc_k, acc_v = carry
        q_blk = lax.dynamic_index_in_dim(q_all, block_id, 0, keepdims=False).astype(jnp.float32)
        d_blk = lax.dynamic_index_in_dim(d_all, block_id, 0, keepdims=False).astype(jnp.float32)
        near_ids = block_id + jnp.arange(-1, 2, dtype=jnp.int32)
        inside = (near_ids >= 0) & (near_ids < BLOCKS)
        near_ids = jnp.clip(near_ids, 0, BLOCKS - 1).astype(jnp.int32)
        k_near = k_all[near_ids].astype(jnp.float32)
        v_near = v_all[near_ids].astype(jnp.float32)
        picked = lax.dynamic_index_in_dim(random_blocks, block_id, 1, keepdims=False).astype(jnp.int32)
        k_rand = k_all[picked, :, head_index, :].astype(jnp.float32)
        v_rand = v_all[picked, :, head_index, :].astype(jnp.float32)
        s_near = jnp.einsum('qhe,tkhe->hqtk', q_blk, k_near) * score_scale
        s_near = jnp.where(inside[None, None, :, None], s_near, MASKED)
        s_glob = jnp.einsum('qhe,gkhe->hqgk', q_blk, k_glob) * score_scale
        s_rand = jnp.einsum('qhe,hrke->hqrk', q_blk, k_rand) * score_scale
        scores = jnp.concatenate([s_near.reshape(HEADS, BLOCK, -1), s_glob.reshape(HEADS, BLOCK, -1), s_rand.reshape(HEADS, BLOCK, -1)], -1)
        row_max = lax.optimization_barrier(jnp.max(scores, -1, keepdims=True))
        exponent = jnp.exp(scores - row_max)
        probs = exponent / lax.optimization_barrier(jnp.sum(exponent, -1, keepdims=True))
        probs_b = rounded(probs)
        p_near, p_glob, p_rand = split_keys(probs_b)
        attended_blk = jnp.einsum('hqtk,tkhe->qhe', p_near, v_near) + jnp.einsum('hqgk,gkhe->qhe', p_glob, v_glob) + jnp.einsum('hqrk,hrke->qhe', p_rand, v_rand)
        g_near = jnp.einsum('qhe,tkhe->hqtk', d_blk, v_near)
        g_glob = jnp.einsum('qhe,gkhe->hqgk', d_blk, v_glob)
        g_rand = jnp.einsum('qhe,hrke->hqrk', d_blk, v_rand)
        grad_probs = jnp.concatenate([g_near.reshape(HEADS, BLOCK, -1), g_glob.reshape(HEADS, BLOCK, -1), g_rand.reshape(HEADS, BLOCK, -1)], -1)
        delta = lax.optimization_barrier(jnp.sum(probs * grad_probs, -1, keepdims=True))
        grad_scores = rounded(probs * (grad_probs - delta))
        ds_near, ds_glob, ds_rand = split_keys(grad_scores)
        grad_q_blk = score_scale * (jnp.einsum('hqtk,tkhe->qhe', ds_near, k_near) + jnp.einsum('hqgk,gkhe->qhe', ds_glob, k_glob) + jnp.einsum('hqrk,hrke->qhe', ds_rand, k_rand))
        acc_k = acc_k.at[near_ids].add(score_scale * jnp.einsum('hqtk,qhe->tkhe', ds_near, q_blk))
        acc_v = acc_v.at[near_ids].add(jnp.einsum('hqtk,qhe->tkhe', p_near, d_blk))
        acc_k = acc_k.at[global_blocks].add(score_scale * jnp.einsum('hqgk,qhe->gkhe', ds_glob, q_blk))
        acc_v = acc_v.at[global_blocks].add(jnp.einsum('hqgk,qhe->gkhe', p_glob, d_blk))
        acc_k = acc_k.at[picked, :, head_index, :].add(rounded(score_scale * jnp.einsum('hqrk,qhe->hrke', ds_rand, q_blk)))
        acc_v = acc_v.at[picked, :, head_index, :].add(rounded(jnp.einsum('hqrk,qhe->hrke', p_rand, d_blk)))
        return ((acc_k, acc_v), (attended_blk.astype(jnp.bfloat16), grad_q_blk.astype(jnp.bfloat16)))
    accumulator = jnp.zeros(block_shape, jnp.float32)
    (acc_k, acc_v), (attended, grad_q) = lax.scan(visit_block, (accumulator, accumulator), jnp.arange(BLOCKS, dtype=jnp.int32))
    return (attended.reshape(LENGTH, WIDTH), grad_q.reshape(LENGTH, WIDTH), acc_k.astype(jnp.bfloat16).reshape(LENGTH, WIDTH), acc_v.astype(jnp.bfloat16).reshape(LENGTH, WIDTH))
```

```python
import functools
import math

import jax
import jax.numpy as jnp
from jax import lax
from jax.experimental import pallas as pl
from jax.experimental.pallas import tpu as pltpu
from jax.sharding import PartitionSpec as P

HEADS = 16
HEAD_DIM = 128
BLOCK = 64
GLOBALS = 2
RANDOM = 3
MASKED = -1e30
MESH = pl.DeviceIdType.MESH
ANY = pl.BlockSpec(memory_space=pl.ANY)
VMEM = pl.BlockSpec(memory_space=pltpu.VMEM)
SMEM = pl.BlockSpec(memory_space=pltpu.SMEM)
VMEM_LIMIT = 48 * 1024 * 1024


def enter(me, shards):
    barrier = pltpu.get_barrier_semaphore()

    def greet(step, carry):
        pl.semaphore_signal(
            barrier, inc=1, device_id={"seq": lax.rem(me + step, shards)}, device_id_type=MESH
        )
        return carry

    lax.fori_loop(1, shards, greet, 0)
    pl.semaphore_wait(barrier, shards - 1)


def remote(src, dst, sems, slot, target):
    return pltpu.make_async_remote_copy(
        src_ref=src,
        dst_ref=dst,
        send_sem=sems[0].at[slot],
        recv_sem=sems[1].at[slot],
        device_id={"seq": target},
        device_id_type=MESH,
    )


def fetch_kernel(shards, capacity, code, k, v, got, before, after, tiles, staged, send, recv, rim_send, rim_recv, own):
    me = lax.axis_index("seq")
    up, down = lax.rem(me + 1, shards), lax.rem(me + shards - 1, shards)
    rows = k.shape[0]
    last = pl.ds(rows - BLOCK, BLOCK)
    initial = pl.ds(0, BLOCK)
    for which, ref in enumerate((k, v)):
        for block in range(rows // BLOCK):
            for head in range(HEADS):
                tiles[block * HEADS + head, which] = ref[
                    block * BLOCK : (block + 1) * BLOCK, head * HEAD_DIM : (head + 1) * HEAD_DIM
                ]
    enter(me, shards)
    rims = []
    for which, ref in enumerate((k, v)):
        rims.append(remote(ref.at[last], before.at[which], (rim_send, rim_recv), which, up))
        rims.append(remote(ref.at[initial], after.at[which], (rim_send, rim_recv), 2 + which, down))

    def gather(target):
        def item(slot, carry):
            staged[target, slot] = tiles[code[target * capacity + slot]]
            return carry

        lax.fori_loop(0, capacity, item, 0)

    def give(step, carry):
        target = lax.rem(me + step, shards)
        gather(target)
        remote(staged.at[target], got.at[me], (send, recv), step, target).start()
        return carry

    lax.fori_loop(1, shards, give, 0)
    for rim in rims:
        rim.start()
    gather(me)
    mine = pltpu.make_async_copy(staged.at[me], got.at[me], own)
    mine.start()
    mine.wait()
    for rim in rims:
        rim.wait()

    def finish(step, carry):
        target = lax.rem(me + step, shards)
        source = lax.rem(me + shards - step, shards)
        remote(staged.at[target], got.at[source], (send, recv), step, target).wait()
        return carry

    lax.fori_loop(1, shards, finish, 0)


def fetch(code, keys, values, shards, capacity):
    kind = jnp.bfloat16
    width = keys.shape[1]
    return pl.pallas_call(
        functools.partial(fetch_kernel, shards, capacity),
        out_shape=(
            jax.ShapeDtypeStruct((shards, capacity, 2, BLOCK, HEAD_DIM), kind),
            jax.ShapeDtypeStruct((2, BLOCK, width), kind),
            jax.ShapeDtypeStruct((2, BLOCK, width), kind),
        ),
        in_specs=[SMEM, VMEM, VMEM],
        out_specs=(ANY, ANY, ANY),
        scratch_shapes=[
            pltpu.VMEM((keys.shape[0] // BLOCK * HEADS, 2, BLOCK, HEAD_DIM), kind),
            pltpu.VMEM((shards, capacity, 2, BLOCK, HEAD_DIM), kind),
            pltpu.SemaphoreType.DMA((shards,)),
            pltpu.SemaphoreType.DMA((shards,)),
            pltpu.SemaphoreType.DMA((4,)),
            pltpu.SemaphoreType.DMA((4,)),
            pltpu.SemaphoreType.DMA,
        ],
        compiler_params=pltpu.CompilerParams(
            collective_id=0, has_side_effects=True, vmem_limit_bytes=VMEM_LIMIT
        ),
        cost_estimate=pl.CostEstimate(flops=0, bytes_accessed=300_000_000, transcendentals=0),
        name="fetch",
    )(code, keys, values)


def give_back_kernel(shards, back, lower, upper, got, above, below, send, recv, rim_send, rim_recv, own):
    me = lax.axis_index("seq")
    up, down = lax.rem(me + 1, shards), lax.rem(me + shards - 1, shards)
    enter(me, shards)
    rims = [
        remote(lower, above, (rim_send, rim_recv), 0, down),
        remote(upper, below, (rim_send, rim_recv), 1, up),
    ]

    def give(step, carry):
        target = lax.rem(me + step, shards)
        remote(back.at[target], got.at[me], (send, recv), step, target).start()
        return carry

    lax.fori_loop(1, shards, give, 0)
    for rim in rims:
        rim.start()
    mine = pltpu.make_async_copy(back.at[me], got.at[me], own)
    mine.start()
    mine.wait()
    for rim in rims:
        rim.wait()

    def finish(step, carry):
        target = lax.rem(me + step, shards)
        source = lax.rem(me + shards - step, shards)
        remote(back.at[target], got.at[source], (send, recv), step, target).wait()
        return carry

    lax.fori_loop(1, shards, finish, 0)


def give_back(back, lower, upper, shards):
    return pl.pallas_call(
        functools.partial(give_back_kernel, shards),
        out_shape=tuple(jax.ShapeDtypeStruct(a.shape, a.dtype) for a in (back, lower, upper)),
        in_specs=[ANY, ANY, ANY],
        out_specs=(ANY, ANY, ANY),
        scratch_shapes=[
            pltpu.SemaphoreType.DMA((shards,)),
            pltpu.SemaphoreType.DMA((shards,)),
            pltpu.SemaphoreType.DMA((2,)),
            pltpu.SemaphoreType.DMA((2,)),
            pltpu.SemaphoreType.DMA,
        ],
        compiler_params=pltpu.CompilerParams(collective_id=1, has_side_effects=True),
        cost_estimate=pl.CostEstimate(flops=0, bytes_accessed=300_000_000, transcendentals=0),
        name="give_back",
    )(back, lower, upper)


def dot(a, b, dims):
    return lax.dot_general(a, b, (dims, ((), ())), preferred_element_type=jnp.float32)


def attend_kernel(blocks, place, owner, rank, q, d, k, v, before, after, glob, *rest):
    items = blocks * RANDOM
    rand = rest[:items]
    attended, grad_q, own_grad, lower, upper, glob_grad, back, near, terms, sems = rest[items:]
    head = pl.program_id(0)
    heads = pl.num_programs(0)
    slot = lax.rem(head, 2)
    scale = 1.0 / math.sqrt(HEAD_DIM)
    n_near = 3 * BLOCK
    n_glob = GLOBALS * BLOCK
    f32, b16 = jnp.float32, jnp.bfloat16

    def out_copy(at_head, at_slot, item):
        index = at_head * items + item
        return pltpu.make_async_copy(
            terms.at[at_slot, item], back.at[owner[index], rank[index]], sems.at[at_slot, item]
        )

    @pl.when(head >= 2)
    def _():
        for item in range(items):
            out_copy(head - 2, slot, item).wait()

    near[...] = jnp.zeros_like(near)
    k_all = jnp.concatenate([before[0], k[...], after[0]], 0)
    v_all = jnp.concatenate([before[1], v[...], after[1]], 0)
    gk, gv = glob[0], glob[1]
    glob_k = jnp.zeros((n_glob, HEAD_DIM), f32)
    glob_v = jnp.zeros((n_glob, HEAD_DIM), f32)
    for j in range(blocks):
        rows = pl.ds(j * BLOCK, BLOCK)
        span = slice(j * BLOCK, j * BLOCK + n_near)
        qj, dj = q[rows, :], d[rows, :]
        picked = [rand[j * RANDOM + r] for r in range(RANDOM)]
        kj = jnp.concatenate([k_all[span], gk] + [x[0, 0, 0] for x in picked], 0)
        vj = jnp.concatenate([v_all[span], gv] + [x[0, 0, 1] for x in picked], 0)
        s = dot(qj, kj, ((1,), (1,))) * scale
        if j == 0 or j == blocks - 1:
            column = lax.broadcasted_iota(jnp.int32, s.shape, 1)
            if j == 0:
                s = jnp.where((column < BLOCK) & (place[0] == 0), MASKED, s)
            if j == blocks - 1:
                outside = (column >= 2 * BLOCK) & (column < n_near) & (place[1] == 0)
                s = jnp.where(outside, MASKED, s)
        e = jnp.exp(s - jnp.max(s, -1, keepdims=True))
        p = e * (1.0 / jnp.sum(e, -1, keepdims=True))
        pb = p.astype(b16)
        attended[rows, :] = dot(pb, vj, ((1,), (0,))).astype(b16)
        gp = dot(dj, vj, ((1,), (1,)))
        delta = jnp.sum(p * gp, -1, keepdims=True)
        ds = (p * (gp - delta)).astype(b16)
        grad_q[rows, :] = (scale * dot(ds, kj, ((1,), (0,)))).astype(b16)
        dk = scale * dot(ds, qj, ((0,), (0,)))
        dv = dot(pb, dj, ((0,), (0,)))
        near[0, span] += dk[:n_near]
        near[1, span] += dv[:n_near]
        glob_k += dk[n_near : n_near + n_glob]
        glob_v += dv[n_near : n_near + n_glob]
        for r in range(RANDOM):
            item = j * RANDOM + r
            at = slice(n_near + n_glob + r * BLOCK, n_near + n_glob + (r + 1) * BLOCK)
            terms[slot, item, 0] = dk[at].astype(b16)
            terms[slot, item, 1] = dv[at].astype(b16)
            out_copy(head, slot, item).start()
    glob_grad[0] = glob_k
    glob_grad[1] = glob_v
    own_grad[...] = near[:, BLOCK : (blocks + 1) * BLOCK]
    lower[...] = near[:, :BLOCK].astype(b16)
    upper[...] = near[:, (blocks + 1) * BLOCK :].astype(b16)

    @pl.when(head == heads - 1)
    def _():
        for item in range(items):
            out_copy(head - 1, 1 - slot, item).wait()
        for item in range(items):
            out_copy(head, slot, item).wait()


def attend(place, owner, rank, q, d, k, v, before, after, glob, got):
    rows, width = q.shape
    blocks = rows // BLOCK
    items = blocks * RANDOM
    f32, b16 = jnp.float32, jnp.bfloat16

    def flat():
        return pl.BlockSpec((rows, HEAD_DIM), lambda h, *_: (0, h))

    def pair(n):
        return pl.BlockSpec((2, n, HEAD_DIM), lambda h, *_: (0, 0, h))

    def picked(item):
        def at(h, place, owner, rank):
            return (owner[h * items + item], rank[h * items + item], 0, 0, 0)

        return pl.BlockSpec((1, 1, 2, BLOCK, HEAD_DIM), at)

    n_glob = GLOBALS * BLOCK
    return pl.pallas_call(
        functools.partial(attend_kernel, blocks),
        grid_spec=pltpu.PrefetchScalarGridSpec(
            num_scalar_prefetch=3,
            grid=(HEADS,),
            in_specs=[flat(), flat(), flat(), flat(), pair(BLOCK), pair(BLOCK), pair(n_glob)]
            + [picked(item) for item in range(items)],
            out_specs=[flat(), flat(), pair(rows), pair(BLOCK), pair(BLOCK), pair(n_glob), ANY],
            scratch_shapes=[
                pltpu.VMEM((2, rows + 2 * BLOCK, HEAD_DIM), f32),
                pltpu.VMEM((2, items, 2, BLOCK, HEAD_DIM), b16),
                pltpu.SemaphoreType.DMA((2, items)),
            ],
        ),
        out_shape=(
            jax.ShapeDtypeStruct((rows, width), b16),
            jax.ShapeDtypeStruct((rows, width), b16),
            jax.ShapeDtypeStruct((2, rows, width), f32),
            jax.ShapeDtypeStruct((2, BLOCK, width), b16),
            jax.ShapeDtypeStruct((2, BLOCK, width), b16),
            jax.ShapeDtypeStruct((2, n_glob, width), f32),
            jax.ShapeDtypeStruct(got.shape, b16),
        ),
        compiler_params=pltpu.CompilerParams(vmem_limit_bytes=VMEM_LIMIT),
        name="attend",
    )(place, owner, rank, q, d, k, v, before, after, glob, *([got] * items))


def combine_kernel(capacity, blocks, code, place, hit, own, above, below, glob, got, grad_k, grad_v, acc):
    source = pl.program_id(0)
    rows = blocks * BLOCK

    @pl.when(source == 0)
    def _():
        acc[...] = own[...]

        @pl.when(place[0] > 0)
        def _():
            acc[:, :BLOCK] += below[...].astype(jnp.float32)

        @pl.when(place[1] > 0)
        def _():
            acc[:, rows - BLOCK :] += above[...].astype(jnp.float32)

        for g in range(GLOBALS):

            @pl.when(hit[g] >= 0)
            def _():
                at = pl.ds(pl.multiple_of(hit[g] * BLOCK, BLOCK), BLOCK)
                acc[:, at] += glob[:, g * BLOCK : (g + 1) * BLOCK]

    for slot in range(capacity):
        packed = code[source * capacity + slot]

        @pl.when(packed >= 0)
        def _():
            row = pl.ds(pl.multiple_of(packed // HEADS * BLOCK, BLOCK), BLOCK)
            column = pl.ds(pl.multiple_of(packed % HEADS * HEAD_DIM, HEAD_DIM), HEAD_DIM)
            acc[:, row, column] += got[0, slot].astype(jnp.float32)

    @pl.when(source == pl.num_programs(0) - 1)
    def _():
        grad_k[...] = acc[0].astype(jnp.bfloat16)
        grad_v[...] = acc[1].astype(jnp.bfloat16)


def combine(code, place, hit, own, above, below, glob, got):
    shards, capacity = got.shape[:2]
    rows, width = own.shape[1:]

    def whole(a):
        return pl.BlockSpec(a.shape, lambda s, *_: (0, 0, 0))

    out = pl.BlockSpec((rows, width), lambda s, *_: (0, 0))
    return pl.pallas_call(
        functools.partial(combine_kernel, capacity, rows // BLOCK),
        grid_spec=pltpu.PrefetchScalarGridSpec(
            num_scalar_prefetch=3,
            grid=(shards,),
            in_specs=[
                whole(own),
                whole(above),
                whole(below),
                whole(glob),
                pl.BlockSpec((1, capacity, 2, BLOCK, HEAD_DIM), lambda s, *_: (s, 0, 0, 0, 0)),
            ],
            out_specs=[out, out],
            scratch_shapes=[pltpu.VMEM((2, rows, width), jnp.float32)],
        ),
        out_shape=(
            jax.ShapeDtypeStruct((rows, width), jnp.bfloat16),
            jax.ShapeDtypeStruct((rows, width), jnp.bfloat16),
        ),
        compiler_params=pltpu.CompilerParams(vmem_limit_bytes=VMEM_LIMIT),
        name="combine",
    )(code, place, hit, own, above, below, glob, got)


def on_device(queries, keys, values, grad_out, global_blocks, random_blocks):
    shards = lax.axis_size("seq")
    me = lax.axis_index("seq")
    blocks = queries.shape[0] // BLOCK
    i32 = jnp.int32

    mine = global_blocks // blocks == me
    parts = []
    for g in range(GLOBALS):
        start = global_blocks[g] % blocks * BLOCK
        pair = jnp.stack(
            [lax.dynamic_slice_in_dim(a, start, BLOCK, 0) for a in (keys, values)], 0
        )
        parts.append(jnp.where(mine[g], pair, jnp.zeros_like(pair)))
    glob = lax.psum(jnp.concatenate(parts, 1), "seq")

    wanted = lax.dynamic_slice_in_dim(random_blocks, me * blocks, blocks, 1).reshape(-1)
    requests = wanted.shape[0]
    capacity = (requests + shards - 1) // shards
    owner = wanted // blocks
    hits = (owner[:, None] == jnp.arange(shards, dtype=i32)[None, :]).astype(i32)
    rank = jnp.sum((jnp.cumsum(hits, 0) - hits) * hits, 1)
    asked = jnp.transpose(random_blocks.reshape(HEADS, shards, blocks, RANDOM), (1, 0, 2, 3))
    asked = asked.reshape(shards, requests)
    served = (asked // blocks == me).astype(i32)
    serve_rank = jnp.cumsum(served, 1) - served
    chosen = served[:, :, None] * (
        serve_rank[:, :, None] == jnp.arange(capacity, dtype=i32)[None, None, :]
    ).astype(i32)
    item_head = jnp.arange(requests, dtype=i32) // (blocks * RANDOM)
    entry = asked % blocks * HEADS + item_head[None, :] + 1
    code = (jnp.sum(chosen * entry[:, :, None], 1) - 1).reshape(-1)

    got, before, after = fetch(jnp.maximum(code, 0), keys, values, shards, capacity)
    place = jnp.stack([me, shards - 1 - me]).astype(i32)
    attended, grad_q, own_grad, lower, upper, glob_grad, back = attend(
        place, owner, rank, queries, grad_out, keys, values, before, after, glob, got
    )
    glob_sum = lax.psum(glob_grad, "seq")
    returned, above, below = give_back(back, lower, upper, shards)
    hit = jnp.where(mine, global_blocks % blocks, -1).astype(i32)
    grad_k, grad_v = combine(code, place, hit, own_grad, above, below, glob_sum, returned)
    return attended, grad_q, grad_k, grad_v


def solution(mesh):
    rows = P(("groups", "seq"), None)
    return jax.shard_map(
        on_device,
        mesh=mesh,
        in_specs=(rows, rows, rows, rows, P("groups"), P("groups", None, None)),
        out_specs=(rows, rows, rows, rows),
        check_vma=False,
    )
```

```python
import functools
import math

import jax
import jax.numpy as jnp
from jax import lax
from jax.experimental import pallas as pl
from jax.experimental.pallas import tpu as pltpu
from jax.sharding import PartitionSpec as P

HEADS = 16
HEAD_DIM = 128
BLOCK = 64
GLOBALS = 2
RANDOM = 3
MASKED = -1e30
INNER = 4
MESH = pl.DeviceIdType.MESH
ANY = pl.BlockSpec(memory_space=pl.ANY)
VMEM = pl.BlockSpec(memory_space=pltpu.VMEM)
SMEM = pl.BlockSpec(memory_space=pltpu.SMEM)
VMEM_LIMIT = 48 * 1024 * 1024


def enter(me, shards):
    barrier = pltpu.get_barrier_semaphore()

    def greet(step, carry):
        pl.semaphore_signal(
            barrier, inc=1, device_id={"seq": lax.rem(me + step, shards)}, device_id_type=MESH
        )
        return carry

    lax.fori_loop(1, shards, greet, 0)
    pl.semaphore_wait(barrier, shards - 1)


def remote(src, dst, sems, slot, target):
    return pltpu.make_async_remote_copy(
        src_ref=src,
        dst_ref=dst,
        send_sem=sems[0].at[slot],
        recv_sem=sems[1].at[slot],
        device_id={"seq": target},
        device_id_type=MESH,
    )


class Share:
    def __init__(self, me, shards, src, out, land_a, quarter, land_b, piece, send, recv, far_send, far_recv, local):
        self.inner, self.outer, self.runs = lax.rem(me, INNER), me // INNER, shards // INNER
        self.src, self.out = src, out
        self.land_a, self.quarter, self.land_b, self.piece = land_a, quarter, land_b, piece
        self.near_sems = [(send.at[i], recv.at[i]) for i in range(2)]
        self.far_sems = [(far_send.at[i], far_recv.at[i]) for i in range(2)]
        self.local = pltpu.make_async_copy(piece, out.at[self.inner, self.outer], local)

    def scatter_near(self, step, wait=False):
        target = lax.rem(self.inner + step, INNER)
        at = lax.rem(self.inner + INNER - step, INNER) if wait else self.inner
        device = self.outer * INNER + target
        return remote(self.src.at[target], self.land_a.at[at], self.near_sems[0], step, device)

    def scatter_far(self, step, wait=False):
        target = lax.rem(self.outer + step, self.runs)
        at = lax.rem(self.outer + self.runs - step, self.runs) if wait else self.outer
        device = target * INNER + self.inner
        return remote(self.quarter.at[target], self.land_b.at[at], self.far_sems[0], step, device)

    def hand_far(self, step, wait=False):
        target = lax.rem(self.outer + step, self.runs)
        at = lax.rem(self.outer + self.runs - step, self.runs) if wait else self.outer
        device = target * INNER + self.inner
        return remote(self.piece, self.out.at[self.inner, at], self.far_sems[1], step, device)

    def hand_near(self, step, wait=False):
        target = lax.rem(self.inner + step, INNER)
        at = lax.rem(self.inner + INNER - step, INNER) if wait else self.inner
        device = self.outer * INNER + target
        return remote(self.out.at[self.inner], self.out.at[at], self.near_sems[1], step, device)

    def start(self, copy, count):
        def one(step, carry):
            copy(step).start()
            return carry

        lax.fori_loop(1, count, one, 0)

    def wait(self, copy, count):
        def one(step, carry):
            copy(step, True).wait()
            return carry

        lax.fori_loop(1, count, one, 0)

    def phase(self, number):
        f32 = jnp.float32
        if number == 0:
            self.start(self.scatter_near, INNER)
        elif number == 1:
            self.wait(self.scatter_near, INNER)
            total = self.src[self.inner].astype(f32)
            for step in range(1, INNER):
                total += self.land_a[lax.rem(self.inner + step, INNER)].astype(f32)
            self.quarter[...] = total.astype(self.quarter.dtype)
            self.start(self.scatter_far, self.runs)
        elif number == 2:
            self.wait(self.scatter_far, self.runs)
            total = lax.fori_loop(
                1,
                self.runs,
                lambda step, t: t + self.land_b[lax.rem(self.outer + step, self.runs)].astype(f32),
                self.quarter[self.outer].astype(f32),
            )
            self.piece[...] = total.astype(self.piece.dtype)
            self.local.start()
            self.start(self.hand_far, self.runs)
        elif number == 3:
            self.local.wait()
            self.wait(self.hand_far, self.runs)
            self.start(self.hand_near, INNER)
        else:
            self.wait(self.hand_near, INNER)


def share_scratch(shape, kind):
    inner, runs = shape[:2]
    return [
        pltpu.VMEM(shape, kind),
        pltpu.VMEM(shape[1:], kind),
        pltpu.VMEM(shape[1:], kind),
        pltpu.VMEM(shape[2:], jnp.bfloat16),
        pltpu.SemaphoreType.DMA((2, inner)),
        pltpu.SemaphoreType.DMA((2, inner)),
        pltpu.SemaphoreType.DMA((2, runs)),
        pltpu.SemaphoreType.DMA((2, runs)),
        pltpu.SemaphoreType.DMA,
    ]


def in_quarters(array, shards):
    return array.reshape(INNER, shards // INNER, array.size // HEAD_DIM // shards, HEAD_DIM)


def fetch_kernel(shards, capacity, code, k, v, glob, got, before, after, glob_out, tiles, staged, send, recv, rim_send, rim_recv, own, *shared):
    me = lax.axis_index("seq")
    up, down = lax.rem(me + 1, shards), lax.rem(me + shards - 1, shards)
    rows = k.shape[0]
    last = pl.ds(rows - BLOCK, BLOCK)
    initial = pl.ds(0, BLOCK)
    enter(me, shards)
    share = Share(me, shards, glob, glob_out, *shared)
    share.phase(0)
    for which, ref in enumerate((k, v)):
        for block in range(rows // BLOCK):
            for head in range(HEADS):
                tiles[block * HEADS + head, which] = ref[
                    block * BLOCK : (block + 1) * BLOCK, head * HEAD_DIM : (head + 1) * HEAD_DIM
                ]
    rims = []
    for which, ref in enumerate((k, v)):
        rims.append(remote(ref.at[last], before.at[which], (rim_send, rim_recv), which, up))
        rims.append(remote(ref.at[initial], after.at[which], (rim_send, rim_recv), 2 + which, down))

    def gather(target):
        def item(slot, carry):
            staged[target, slot] = tiles[code[target * capacity + slot]]
            return carry

        lax.fori_loop(0, capacity, item, 0)

    def give(step, carry):
        target = lax.rem(me + step, shards)
        gather(target)
        remote(staged.at[target], got.at[me], (send, recv), step, target).start()
        return carry

    for part in range(4):
        lax.fori_loop(max(1, shards * part // 4), shards * (part + 1) // 4, give, 0)
        if part < 3:
            share.phase(part + 1)
    for rim in rims:
        rim.start()
    gather(me)
    mine = pltpu.make_async_copy(staged.at[me], got.at[me], own)
    mine.start()
    mine.wait()
    for rim in rims:
        rim.wait()

    def finish(step, carry):
        target = lax.rem(me + step, shards)
        source = lax.rem(me + shards - step, shards)
        remote(staged.at[target], got.at[source], (send, recv), step, target).wait()
        return carry

    lax.fori_loop(1, shards, finish, 0)
    share.phase(4)


def fetch(code, keys, values, glob, shards, capacity):
    kind = jnp.bfloat16
    width = keys.shape[1]
    return pl.pallas_call(
        functools.partial(fetch_kernel, shards, capacity),
        out_shape=(
            jax.ShapeDtypeStruct((shards, capacity, 2, BLOCK, HEAD_DIM), kind),
            jax.ShapeDtypeStruct((2, BLOCK, width), kind),
            jax.ShapeDtypeStruct((2, BLOCK, width), kind),
            jax.ShapeDtypeStruct(glob.shape, kind),
        ),
        in_specs=[SMEM, VMEM, VMEM, VMEM],
        out_specs=(ANY, ANY, ANY, ANY),
        scratch_shapes=[
            pltpu.VMEM((keys.shape[0] // BLOCK * HEADS, 2, BLOCK, HEAD_DIM), kind),
            pltpu.VMEM((shards, capacity, 2, BLOCK, HEAD_DIM), kind),
            pltpu.SemaphoreType.DMA((shards,)),
            pltpu.SemaphoreType.DMA((shards,)),
            pltpu.SemaphoreType.DMA((4,)),
            pltpu.SemaphoreType.DMA((4,)),
            pltpu.SemaphoreType.DMA,
        ]
        + share_scratch(glob.shape, kind),
        compiler_params=pltpu.CompilerParams(
            collective_id=0, has_side_effects=True, vmem_limit_bytes=VMEM_LIMIT
        ),
        cost_estimate=pl.CostEstimate(flops=0, bytes_accessed=300_000_000, transcendentals=0),
        name="fetch",
    )(code, keys, values, glob)


def give_back_kernel(
    shards, back, lower, upper, glob, got, above, below, glob_out, send, recv, rim_send, rim_recv, own, *shared
):
    me = lax.axis_index("seq")
    up, down = lax.rem(me + 1, shards), lax.rem(me + shards - 1, shards)
    enter(me, shards)
    share = Share(me, shards, glob, glob_out, *shared)
    share.phase(0)
    rims = [
        remote(lower, above, (rim_send, rim_recv), 0, down),
        remote(upper, below, (rim_send, rim_recv), 1, up),
    ]

    def give(step, carry):
        target = lax.rem(me + step, shards)
        remote(back.at[target], got.at[me], (send, recv), step, target).start()
        return carry

    for part in range(4):
        lax.fori_loop(max(1, shards * part // 4), shards * (part + 1) // 4, give, 0)
        if part < 3:
            share.phase(part + 1)
    for rim in rims:
        rim.start()
    mine = pltpu.make_async_copy(back.at[me], got.at[me], own)
    mine.start()
    mine.wait()
    for rim in rims:
        rim.wait()

    def finish(step, carry):
        target = lax.rem(me + step, shards)
        source = lax.rem(me + shards - step, shards)
        remote(back.at[target], got.at[source], (send, recv), step, target).wait()
        return carry

    lax.fori_loop(1, shards, finish, 0)
    share.phase(4)


def give_back(back, lower, upper, glob, shards):
    return pl.pallas_call(
        functools.partial(give_back_kernel, shards),
        out_shape=tuple(jax.ShapeDtypeStruct(a.shape, jnp.bfloat16) for a in (back, lower, upper, glob)),
        in_specs=[ANY, ANY, ANY, VMEM],
        out_specs=(ANY, ANY, ANY, ANY),
        scratch_shapes=[
            pltpu.SemaphoreType.DMA((shards,)),
            pltpu.SemaphoreType.DMA((shards,)),
            pltpu.SemaphoreType.DMA((2,)),
            pltpu.SemaphoreType.DMA((2,)),
            pltpu.SemaphoreType.DMA,
        ]
        + share_scratch(glob.shape, glob.dtype),
        compiler_params=pltpu.CompilerParams(
            collective_id=1, has_side_effects=True, vmem_limit_bytes=VMEM_LIMIT
        ),
        cost_estimate=pl.CostEstimate(flops=0, bytes_accessed=300_000_000, transcendentals=0),
        name="give_back",
    )(back, lower, upper, glob)


def dot(a, b, dims):
    return lax.dot_general(a, b, (dims, ((), ())), preferred_element_type=jnp.float32)


def attend_kernel(blocks, place, owner, rank, q, d, k, v, before, after, glob, *rest):
    items = blocks * RANDOM
    rand = rest[:items]
    attended, grad_q, own_grad, lower, upper, glob_grad, back, near, terms, sems = rest[items:]
    head = pl.program_id(0)
    heads = pl.num_programs(0)
    slot = lax.rem(head, 2)
    scale = 1.0 / math.sqrt(HEAD_DIM)
    n_near = 3 * BLOCK
    n_glob = GLOBALS * BLOCK
    f32, b16 = jnp.float32, jnp.bfloat16

    def out_copy(at_head, at_slot, item):
        index = at_head * items + item
        return pltpu.make_async_copy(
            terms.at[at_slot, item], back.at[owner[index], rank[index]], sems.at[at_slot, item]
        )

    @pl.when(head >= 2)
    def _():
        for item in range(items):
            out_copy(head - 2, slot, item).wait()

    near[...] = jnp.zeros_like(near)
    k_all = jnp.concatenate([before[0], k[...], after[0]], 0)
    v_all = jnp.concatenate([before[1], v[...], after[1]], 0)
    gk, gv = glob[0, 0], glob[0, 1]
    each = range(blocks)
    rows = [slice(j * BLOCK, (j + 1) * BLOCK) for j in each]
    span = [slice(j * BLOCK, j * BLOCK + n_near) for j in each]
    picked = [[rand[j * RANDOM + r] for r in range(RANDOM)] for j in each]
    qs = [q[rows[j], :] for j in each]
    gs = [d[rows[j], :] for j in each]
    ks = [jnp.concatenate([k_all[span[j]], gk] + [x[0, 0, 0] for x in picked[j]], 0) for j in each]
    vs = [jnp.concatenate([v_all[span[j]], gv] + [x[0, 0, 1] for x in picked[j]], 0) for j in each]
    scores = [dot(qs[j], ks[j], ((1,), (1,))) * scale for j in each]
    gps = [dot(gs[j], vs[j], ((1,), (1,))) for j in each]
    column = lax.broadcasted_iota(jnp.int32, scores[0].shape, 1)
    scores[0] = jnp.where((column < BLOCK) & (place[0] == 0), MASKED, scores[0])
    outside = (column >= 2 * BLOCK) & (column < n_near) & (place[1] == 0)
    scores[-1] = jnp.where(outside, MASKED, scores[-1])
    es = [jnp.exp(x - jnp.max(x, -1, keepdims=True)) for x in scores]
    ps = [x * (1.0 / jnp.sum(x, -1, keepdims=True)) for x in es]
    pbs = [x.astype(b16) for x in ps]
    deltas = [jnp.sum(ps[j] * gps[j], -1, keepdims=True) for j in each]
    dss = [(ps[j] * (gps[j] - deltas[j])).astype(b16) for j in each]
    dks = [scale * dot(dss[j], qs[j], ((0,), (0,))) for j in each]
    dvs = [dot(pbs[j], gs[j], ((0,), (0,))) for j in each]
    outs = [dot(pbs[j], vs[j], ((1,), (0,))).astype(b16) for j in each]
    gqs = [(scale * dot(dss[j], ks[j], ((1,), (0,)))).astype(b16) for j in each]
    for j in each:
        for r in range(RANDOM):
            item = j * RANDOM + r
            at = slice(n_near + n_glob + r * BLOCK, n_near + n_glob + (r + 1) * BLOCK)
            terms[slot, item, 0] = dks[j][at].astype(b16)
            terms[slot, item, 1] = dvs[j][at].astype(b16)
    for item in range(items):
        out_copy(head, slot, item).start()
    for j in each:
        attended[rows[j], :] = outs[j]
        grad_q[rows[j], :] = gqs[j]
        near[0, span[j]] += dks[j][:n_near]
        near[1, span[j]] += dvs[j][:n_near]
    glob_grad[0, 0] = sum(x[n_near : n_near + n_glob] for x in dks)
    glob_grad[0, 1] = sum(x[n_near : n_near + n_glob] for x in dvs)
    own_grad[...] = near[:, BLOCK : (blocks + 1) * BLOCK]
    lower[...] = near[:, :BLOCK].astype(b16)
    upper[...] = near[:, (blocks + 1) * BLOCK :].astype(b16)

    @pl.when(head == heads - 1)
    def _():
        for item in range(items):
            out_copy(head - 1, 1 - slot, item).wait()
        for item in range(items):
            out_copy(head, slot, item).wait()


def attend(place, owner, rank, q, d, k, v, before, after, glob, got):
    rows, width = q.shape
    blocks = rows // BLOCK
    items = blocks * RANDOM
    f32, b16 = jnp.float32, jnp.bfloat16

    def flat():
        return pl.BlockSpec((rows, HEAD_DIM), lambda h, *_: (0, h))

    def pair(n):
        return pl.BlockSpec((2, n, HEAD_DIM), lambda h, *_: (0, 0, h))

    def picked(item):
        def at(h, place, owner, rank):
            return (owner[h * items + item], rank[h * items + item], 0, 0, 0)

        return pl.BlockSpec((1, 1, 2, BLOCK, HEAD_DIM), at)

    n_glob = GLOBALS * BLOCK
    shared = pl.BlockSpec((1, 2, n_glob, HEAD_DIM), lambda h, *_: (h, 0, 0, 0))
    return pl.pallas_call(
        functools.partial(attend_kernel, blocks),
        grid_spec=pltpu.PrefetchScalarGridSpec(
            num_scalar_prefetch=3,
            grid=(HEADS,),
            in_specs=[flat(), flat(), flat(), flat(), pair(BLOCK), pair(BLOCK), shared]
            + [picked(item) for item in range(items)],
            out_specs=[flat(), flat(), pair(rows), pair(BLOCK), pair(BLOCK), shared, ANY],
            scratch_shapes=[
                pltpu.VMEM((2, rows + 2 * BLOCK, HEAD_DIM), f32),
                pltpu.VMEM((2, items, 2, BLOCK, HEAD_DIM), b16),
                pltpu.SemaphoreType.DMA((2, items)),
            ],
        ),
        out_shape=(
            jax.ShapeDtypeStruct((rows, width), b16),
            jax.ShapeDtypeStruct((rows, width), b16),
            jax.ShapeDtypeStruct((2, rows, width), f32),
            jax.ShapeDtypeStruct((2, BLOCK, width), b16),
            jax.ShapeDtypeStruct((2, BLOCK, width), b16),
            jax.ShapeDtypeStruct(glob.shape, f32),
            jax.ShapeDtypeStruct(got.shape, b16),
        ),
        compiler_params=pltpu.CompilerParams(vmem_limit_bytes=VMEM_LIMIT),
        name="attend",
    )(place, owner, rank, q, d, k, v, before, after, glob, *([got] * items))


def combine_kernel(capacity, blocks, code, place, hit, own, above, below, glob, got, grad_k, grad_v, acc):
    source = pl.program_id(0)
    rows = blocks * BLOCK

    @pl.when(source == 0)
    def _():
        acc[...] = own[...]

        @pl.when(place[0] > 0)
        def _():
            acc[:, :BLOCK] += below[...].astype(jnp.float32)

        @pl.when(place[1] > 0)
        def _():
            acc[:, rows - BLOCK :] += above[...].astype(jnp.float32)

        for g in range(GLOBALS):

            @pl.when(hit[g] >= 0)
            def _():
                at = pl.ds(pl.multiple_of(hit[g] * BLOCK, BLOCK), BLOCK)
                for head in range(HEADS):
                    column = slice(head * HEAD_DIM, (head + 1) * HEAD_DIM)
                    acc[:, at, column] += glob[head, :, g * BLOCK : (g + 1) * BLOCK].astype(jnp.float32)

    for slot in range(capacity):
        packed = code[source * capacity + slot]

        @pl.when(packed >= 0)
        def _():
            row = pl.ds(pl.multiple_of(packed // HEADS * BLOCK, BLOCK), BLOCK)
            column = pl.ds(pl.multiple_of(packed % HEADS * HEAD_DIM, HEAD_DIM), HEAD_DIM)
            acc[:, row, column] += got[0, slot].astype(jnp.float32)

    @pl.when(source == pl.num_programs(0) - 1)
    def _():
        grad_k[...] = acc[0].astype(jnp.bfloat16)
        grad_v[...] = acc[1].astype(jnp.bfloat16)


def combine(code, place, hit, own, above, below, glob, got):
    shards, capacity = got.shape[:2]
    rows, width = own.shape[1:]

    def whole(a):
        return pl.BlockSpec(a.shape, lambda s, *_: (0,) * a.ndim)

    out = pl.BlockSpec((rows, width), lambda s, *_: (0, 0))
    return pl.pallas_call(
        functools.partial(combine_kernel, capacity, rows // BLOCK),
        grid_spec=pltpu.PrefetchScalarGridSpec(
            num_scalar_prefetch=3,
            grid=(shards,),
            in_specs=[
                whole(own),
                whole(above),
                whole(below),
                whole(glob),
                pl.BlockSpec((1, capacity, 2, BLOCK, HEAD_DIM), lambda s, *_: (s, 0, 0, 0, 0)),
            ],
            out_specs=[out, out],
            scratch_shapes=[pltpu.VMEM((2, rows, width), jnp.float32)],
        ),
        out_shape=(
            jax.ShapeDtypeStruct((rows, width), jnp.bfloat16),
            jax.ShapeDtypeStruct((rows, width), jnp.bfloat16),
        ),
        compiler_params=pltpu.CompilerParams(vmem_limit_bytes=VMEM_LIMIT),
        name="combine",
    )(code, place, hit, own, above, below, glob, got)


def on_device(queries, keys, values, grad_out, global_blocks, random_blocks):
    shards = lax.axis_size("seq")
    me = lax.axis_index("seq")
    blocks = queries.shape[0] // BLOCK
    i32 = jnp.int32

    mine = global_blocks // blocks == me
    parts = []
    for g in range(GLOBALS):
        start = global_blocks[g] % blocks * BLOCK
        pair = jnp.stack(
            [lax.dynamic_slice_in_dim(a, start, BLOCK, 0) for a in (keys, values)], 0
        )
        parts.append(jnp.where(mine[g], pair, jnp.zeros_like(pair)))
    glob = jnp.concatenate(parts, 1).reshape(2, GLOBALS * BLOCK, HEADS, HEAD_DIM)
    glob = jnp.transpose(glob, (2, 0, 1, 3))

    wanted = lax.dynamic_slice_in_dim(random_blocks, me * blocks, blocks, 1).reshape(-1)
    requests = wanted.shape[0]
    capacity = (requests + shards - 1) // shards
    owner = wanted // blocks
    hits = (owner[:, None] == jnp.arange(shards, dtype=i32)[None, :]).astype(i32)
    rank = jnp.sum((jnp.cumsum(hits, 0) - hits) * hits, 1)
    asked = jnp.transpose(random_blocks.reshape(HEADS, shards, blocks, RANDOM), (1, 0, 2, 3))
    asked = asked.reshape(shards, requests)
    served = (asked // blocks == me).astype(i32)
    serve_rank = jnp.cumsum(served, 1) - served
    chosen = served[:, :, None] * (
        serve_rank[:, :, None] == jnp.arange(capacity, dtype=i32)[None, None, :]
    ).astype(i32)
    item_head = jnp.arange(requests, dtype=i32) // (blocks * RANDOM)
    entry = asked % blocks * HEADS + item_head[None, :] + 1
    code = (jnp.sum(chosen * entry[:, :, None], 1) - 1).reshape(-1)

    got, before, after, glob_all = fetch(
        jnp.maximum(code, 0), keys, values, in_quarters(glob, shards), shards, capacity
    )
    glob = glob_all.reshape(glob.shape)
    place = jnp.stack([me, shards - 1 - me]).astype(i32)
    attended, grad_q, own_grad, lower, upper, glob_grad, back = attend(
        place, owner, rank, queries, grad_out, keys, values, before, after, glob, got
    )
    returned, above, below, glob_sum = give_back(
        back, lower, upper, in_quarters(glob_grad, shards), shards
    )
    glob_sum = glob_sum.reshape(glob.shape)
    hit = jnp.where(mine, global_blocks % blocks, -1).astype(i32)
    grad_k, grad_v = combine(code, place, hit, own_grad, above, below, glob_sum, returned)
    return attended, grad_q, grad_k, grad_v


def solution(mesh):
    rows = P(("groups", "seq"), None)
    return jax.shard_map(
        on_device,
        mesh=mesh,
        in_specs=(rows, rows, rows, rows, P("groups"), P("groups", None, None)),
        out_specs=(rows, rows, rows, rows),
        check_vma=False,
    )
```

```python
import functools
import math

import jax
import jax.numpy as jnp
from jax import lax
from jax.experimental import pallas as pl
from jax.experimental.pallas import tpu as pltpu
from jax.sharding import PartitionSpec as P

HEADS = 16
HEAD_DIM = 128
BLOCK = 64
GLOBALS = 2
RANDOM = 3
MASKED = -1e30
INNER = 4
MESH = pl.DeviceIdType.MESH
ANY = pl.BlockSpec(memory_space=pl.ANY)
VMEM = pl.BlockSpec(memory_space=pltpu.VMEM)
SMEM = pl.BlockSpec(memory_space=pltpu.SMEM)
VMEM_LIMIT = 48 * 1024 * 1024


def enter(me, shards):
    barrier = pltpu.get_barrier_semaphore()

    def greet(step, carry):
        pl.semaphore_signal(
            barrier, inc=1, device_id={"seq": lax.rem(me + step, shards)}, device_id_type=MESH
        )
        return carry

    lax.fori_loop(1, shards, greet, 0)
    pl.semaphore_wait(barrier, shards - 1)


def remote(src, dst, sems, slot, target):
    return pltpu.make_async_remote_copy(
        src_ref=src,
        dst_ref=dst,
        send_sem=sems[0].at[slot],
        recv_sem=sems[1].at[slot],
        device_id={"seq": target},
        device_id_type=MESH,
    )


class Share:
    def __init__(self, me, shards, src, out, land_a, quarter, land_b, piece, send, recv, far_send, far_recv, local):
        self.inner, self.outer, self.runs = lax.rem(me, INNER), me // INNER, shards // INNER
        self.src, self.out = src, out
        self.land_a, self.quarter, self.land_b, self.piece = land_a, quarter, land_b, piece
        self.near_sems = [(send.at[i], recv.at[i]) for i in range(2)]
        self.far_sems = [(far_send.at[i], far_recv.at[i]) for i in range(2)]
        self.local = pltpu.make_async_copy(piece, out.at[self.inner, self.outer], local)

    def scatter_near(self, step, wait=False):
        target = lax.rem(self.inner + step, INNER)
        at = lax.rem(self.inner + INNER - step, INNER) if wait else self.inner
        device = self.outer * INNER + target
        return remote(self.src.at[target], self.land_a.at[at], self.near_sems[0], step, device)

    def scatter_far(self, step, wait=False):
        target = lax.rem(self.outer + step, self.runs)
        at = lax.rem(self.outer + self.runs - step, self.runs) if wait else self.outer
        device = target * INNER + self.inner
        return remote(self.quarter.at[target], self.land_b.at[at], self.far_sems[0], step, device)

    def hand_far(self, step, wait=False):
        target = lax.rem(self.outer + step, self.runs)
        at = lax.rem(self.outer + self.runs - step, self.runs) if wait else self.outer
        device = target * INNER + self.inner
        return remote(self.piece, self.out.at[self.inner, at], self.far_sems[1], step, device)

    def hand_near(self, step, wait=False):
        target = lax.rem(self.inner + step, INNER)
        at = lax.rem(self.inner + INNER - step, INNER) if wait else self.inner
        device = self.outer * INNER + target
        return remote(self.out.at[self.inner], self.out.at[at], self.near_sems[1], step, device)

    def start(self, copy, count):
        def one(step, carry):
            copy(step).start()
            return carry

        lax.fori_loop(1, count, one, 0)

    def wait(self, copy, count):
        def one(step, carry):
            copy(step, True).wait()
            return carry

        lax.fori_loop(1, count, one, 0)

    def phase(self, number):
        f32 = jnp.float32
        if number == 0:
            self.start(self.scatter_near, INNER)
        elif number == 1:
            self.wait(self.scatter_near, INNER)
            total = self.src[self.inner].astype(f32)
            for step in range(1, INNER):
                total += self.land_a[lax.rem(self.inner + step, INNER)].astype(f32)
            self.quarter[...] = total.astype(self.quarter.dtype)
            self.start(self.scatter_far, self.runs)
        elif number == 2:
            self.wait(self.scatter_far, self.runs)
            total = lax.fori_loop(
                1,
                self.runs,
                lambda step, t: t + self.land_b[lax.rem(self.outer + step, self.runs)].astype(f32),
                self.quarter[self.outer].astype(f32),
            )
            self.piece[...] = total.astype(self.piece.dtype)
            self.local.start()
            self.start(self.hand_far, self.runs)
        elif number == 3:
            self.local.wait()
            self.wait(self.hand_far, self.runs)
            self.start(self.hand_near, INNER)
        else:
            self.wait(self.hand_near, INNER)


def share_scratch(shape, kind):
    inner, runs = shape[:2]
    return [
        pltpu.VMEM(shape, kind),
        pltpu.VMEM(shape[1:], kind),
        pltpu.VMEM(shape[1:], kind),
        pltpu.VMEM(shape[2:], jnp.bfloat16),
        pltpu.SemaphoreType.DMA((2, inner)),
        pltpu.SemaphoreType.DMA((2, inner)),
        pltpu.SemaphoreType.DMA((2, runs)),
        pltpu.SemaphoreType.DMA((2, runs)),
        pltpu.SemaphoreType.DMA,
    ]


def in_quarters(array, shards):
    return array.reshape(INNER, shards // INNER, array.size // HEAD_DIM // shards, HEAD_DIM)


def fetch_kernel(shards, capacity, code, k, v, glob, got, before, after, glob_out, tiles, staged, send, recv, rim_send, rim_recv, own, *shared):
    me = lax.axis_index("seq")
    up, down = lax.rem(me + 1, shards), lax.rem(me + shards - 1, shards)
    rows = k.shape[0]
    last = pl.ds(rows - BLOCK, BLOCK)
    initial = pl.ds(0, BLOCK)
    enter(me, shards)
    share = Share(me, shards, glob, glob_out, *shared)
    share.phase(0)
    for which, ref in enumerate((k, v)):
        for block in range(rows // BLOCK):
            for head in range(HEADS):
                tiles[block * HEADS + head, which] = ref[
                    block * BLOCK : (block + 1) * BLOCK, head * HEAD_DIM : (head + 1) * HEAD_DIM
                ]
    rims = []
    for which, ref in enumerate((k, v)):
        rims.append(remote(ref.at[last], before.at[which], (rim_send, rim_recv), which, up))
        rims.append(remote(ref.at[initial], after.at[which], (rim_send, rim_recv), 2 + which, down))

    def gather(target):
        def item(slot, carry):
            staged[target, slot] = tiles[code[target * capacity + slot]]
            return carry

        lax.fori_loop(0, capacity, item, 0)

    def give(step, carry):
        step = lax.rem(step * (shards // 2 - 1), shards)
        target = lax.rem(me + step, shards)
        gather(target)
        remote(staged.at[target], got.at[me], (send, recv), step, target).start()
        return carry

    for part in range(8):
        lax.fori_loop(max(1, shards * part // 8), shards * (part + 1) // 8, give, 0)
        if part < 3:
            share.phase(part + 1)
    for rim in rims:
        rim.start()
    gather(me)
    mine = pltpu.make_async_copy(staged.at[me], got.at[me], own)
    mine.start()
    mine.wait()
    for rim in rims:
        rim.wait()

    def finish(step, carry):
        step = lax.rem(step * (shards // 2 - 1), shards)
        target = lax.rem(me + step, shards)
        source = lax.rem(me + shards - step, shards)
        remote(staged.at[target], got.at[source], (send, recv), step, target).wait()
        return carry

    lax.fori_loop(1, shards, finish, 0)
    share.phase(4)


def fetch(code, keys, values, glob, shards, capacity):
    kind = jnp.bfloat16
    width = keys.shape[1]
    return pl.pallas_call(
        functools.partial(fetch_kernel, shards, capacity),
        out_shape=(
            jax.ShapeDtypeStruct((shards, capacity, 2, BLOCK, HEAD_DIM), kind),
            jax.ShapeDtypeStruct((2, BLOCK, width), kind),
            jax.ShapeDtypeStruct((2, BLOCK, width), kind),
            jax.ShapeDtypeStruct(glob.shape, kind),
        ),
        in_specs=[SMEM, VMEM, VMEM, VMEM],
        out_specs=(ANY, ANY, ANY, ANY),
        scratch_shapes=[
            pltpu.VMEM((keys.shape[0] // BLOCK * HEADS, 2, BLOCK, HEAD_DIM), kind),
            pltpu.VMEM((shards, capacity, 2, BLOCK, HEAD_DIM), kind),
            pltpu.SemaphoreType.DMA((shards,)),
            pltpu.SemaphoreType.DMA((shards,)),
            pltpu.SemaphoreType.DMA((4,)),
            pltpu.SemaphoreType.DMA((4,)),
            pltpu.SemaphoreType.DMA,
        ]
        + share_scratch(glob.shape, kind),
        compiler_params=pltpu.CompilerParams(
            collective_id=0, has_side_effects=True, vmem_limit_bytes=VMEM_LIMIT
        ),
        cost_estimate=pl.CostEstimate(flops=0, bytes_accessed=300_000_000, transcendentals=0),
        name="fetch",
    )(code, keys, values, glob)


def give_back_kernel(
    shards, back, lower, upper, glob, got, above, below, glob_out, send, recv, rim_send, rim_recv, own, *shared
):
    me = lax.axis_index("seq")
    up, down = lax.rem(me + 1, shards), lax.rem(me + shards - 1, shards)
    enter(me, shards)
    share = Share(me, shards, glob, glob_out, *shared)
    share.phase(0)
    rims = [
        remote(lower, above, (rim_send, rim_recv), 0, down),
        remote(upper, below, (rim_send, rim_recv), 1, up),
    ]

    def give(step, carry):
        step = lax.rem(step * (shards // 2 - 1), shards)
        target = lax.rem(me + step, shards)
        remote(back.at[target], got.at[me], (send, recv), step, target).start()
        return carry

    for part in range(4):
        lax.fori_loop(max(1, shards * part // 4), shards * (part + 1) // 4, give, 0)
        if part < 3:
            share.phase(part + 1)
    for rim in rims:
        rim.start()
    mine = pltpu.make_async_copy(back.at[me], got.at[me], own)
    mine.start()
    mine.wait()
    for rim in rims:
        rim.wait()

    def finish(step, carry):
        step = lax.rem(step * (shards // 2 - 1), shards)
        target = lax.rem(me + step, shards)
        source = lax.rem(me + shards - step, shards)
        remote(back.at[target], got.at[source], (send, recv), step, target).wait()
        return carry

    lax.fori_loop(1, shards, finish, 0)
    share.phase(4)


def give_back(back, lower, upper, glob, shards):
    return pl.pallas_call(
        functools.partial(give_back_kernel, shards),
        out_shape=tuple(jax.ShapeDtypeStruct(a.shape, jnp.bfloat16) for a in (back, lower, upper, glob)),
        in_specs=[ANY, ANY, ANY, VMEM],
        out_specs=(ANY, ANY, ANY, ANY),
        scratch_shapes=[
            pltpu.SemaphoreType.DMA((shards,)),
            pltpu.SemaphoreType.DMA((shards,)),
            pltpu.SemaphoreType.DMA((2,)),
            pltpu.SemaphoreType.DMA((2,)),
            pltpu.SemaphoreType.DMA,
        ]
        + share_scratch(glob.shape, glob.dtype),
        compiler_params=pltpu.CompilerParams(
            collective_id=1, has_side_effects=True, vmem_limit_bytes=VMEM_LIMIT
        ),
        cost_estimate=pl.CostEstimate(flops=0, bytes_accessed=300_000_000, transcendentals=0),
        name="give_back",
    )(back, lower, upper, glob)


def dot(a, b, dims):
    return lax.dot_general(a, b, (dims, ((), ())), preferred_element_type=jnp.float32)


def attend_kernel(blocks, place, owner, rank, q, d, k, v, before, after, glob, *rest):
    items = blocks * RANDOM
    rand = rest[:items]
    attended, grad_q, own_grad, lower, upper, glob_grad, back, near, terms, sems = rest[items:]
    head = pl.program_id(0)
    heads = pl.num_programs(0)
    slot = lax.rem(head, 2)
    scale = 1.0 / math.sqrt(HEAD_DIM)
    n_near = 3 * BLOCK
    n_glob = GLOBALS * BLOCK
    f32, b16 = jnp.float32, jnp.bfloat16

    def out_copy(at_head, at_slot, item):
        index = at_head * items + item
        return pltpu.make_async_copy(
            terms.at[at_slot, item], back.at[owner[index], rank[index]], sems.at[at_slot, item]
        )

    @pl.when(head >= 2)
    def _():
        for item in range(items):
            out_copy(head - 2, slot, item).wait()

    near[...] = jnp.zeros_like(near)
    k_all = jnp.concatenate([before[0], k[...], after[0]], 0)
    v_all = jnp.concatenate([before[1], v[...], after[1]], 0)
    gk, gv = glob[0, 0], glob[0, 1]
    each = range(blocks)
    rows = [slice(j * BLOCK, (j + 1) * BLOCK) for j in each]
    span = [slice(j * BLOCK, j * BLOCK + n_near) for j in each]
    picked = [[rand[j * RANDOM + r] for r in range(RANDOM)] for j in each]
    qs = [q[rows[j], :] for j in each]
    gs = [d[rows[j], :] for j in each]
    ks = [jnp.concatenate([k_all[span[j]], gk] + [x[0, 0, 0] for x in picked[j]], 0) for j in each]
    vs = [jnp.concatenate([v_all[span[j]], gv] + [x[0, 0, 1] for x in picked[j]], 0) for j in each]
    scores = [dot(qs[j], ks[j], ((1,), (1,))) * scale for j in each]
    gps = [dot(gs[j], vs[j], ((1,), (1,))) for j in each]
    column = lax.broadcasted_iota(jnp.int32, scores[0].shape, 1)
    scores[0] = jnp.where((column < BLOCK) & (place[0] == 0), MASKED, scores[0])
    outside = (column >= 2 * BLOCK) & (column < n_near) & (place[1] == 0)
    scores[-1] = jnp.where(outside, MASKED, scores[-1])
    es = [jnp.exp(x - jnp.max(x, -1, keepdims=True)) for x in scores]
    ps = [x * (1.0 / jnp.sum(x, -1, keepdims=True)) for x in es]
    pbs = [x.astype(b16) for x in ps]
    deltas = [jnp.sum(ps[j] * gps[j], -1, keepdims=True) for j in each]
    dss = [(ps[j] * (gps[j] - deltas[j])).astype(b16) for j in each]
    dks = [scale * dot(dss[j], qs[j], ((0,), (0,))) for j in each]
    dvs = [dot(pbs[j], gs[j], ((0,), (0,))) for j in each]
    outs = [dot(pbs[j], vs[j], ((1,), (0,))).astype(b16) for j in each]
    gqs = [(scale * dot(dss[j], ks[j], ((1,), (0,)))).astype(b16) for j in each]
    for j in each:
        for r in range(RANDOM):
            item = j * RANDOM + r
            at = slice(n_near + n_glob + r * BLOCK, n_near + n_glob + (r + 1) * BLOCK)
            terms[slot, item, 0] = dks[j][at].astype(b16)
            terms[slot, item, 1] = dvs[j][at].astype(b16)
    for item in range(items):
        out_copy(head, slot, item).start()
    for j in each:
        attended[rows[j], :] = outs[j]
        grad_q[rows[j], :] = gqs[j]
        near[0, span[j]] += dks[j][:n_near]
        near[1, span[j]] += dvs[j][:n_near]
    glob_grad[0, 0] = sum(x[n_near : n_near + n_glob] for x in dks)
    glob_grad[0, 1] = sum(x[n_near : n_near + n_glob] for x in dvs)
    own_grad[...] = near[:, BLOCK : (blocks + 1) * BLOCK]
    lower[...] = near[:, :BLOCK].astype(b16)
    upper[...] = near[:, (blocks + 1) * BLOCK :].astype(b16)

    @pl.when(head == heads - 1)
    def _():
        for item in range(items):
            out_copy(head - 1, 1 - slot, item).wait()
        for item in range(items):
            out_copy(head, slot, item).wait()


def attend(place, owner, rank, q, d, k, v, before, after, glob, got):
    rows, width = q.shape
    blocks = rows // BLOCK
    items = blocks * RANDOM
    f32, b16 = jnp.float32, jnp.bfloat16

    def flat():
        return pl.BlockSpec((rows, HEAD_DIM), lambda h, *_: (0, h))

    def pair(n):
        return pl.BlockSpec((2, n, HEAD_DIM), lambda h, *_: (0, 0, h))

    def picked(item):
        def at(h, place, owner, rank):
            return (owner[h * items + item], rank[h * items + item], 0, 0, 0)

        return pl.BlockSpec((1, 1, 2, BLOCK, HEAD_DIM), at)

    n_glob = GLOBALS * BLOCK
    shared = pl.BlockSpec((1, 2, n_glob, HEAD_DIM), lambda h, *_: (h, 0, 0, 0))
    return pl.pallas_call(
        functools.partial(attend_kernel, blocks),
        grid_spec=pltpu.PrefetchScalarGridSpec(
            num_scalar_prefetch=3,
            grid=(HEADS,),
            in_specs=[flat(), flat(), flat(), flat(), pair(BLOCK), pair(BLOCK), shared]
            + [picked(item) for item in range(items)],
            out_specs=[flat(), flat(), pair(rows), pair(BLOCK), pair(BLOCK), shared, ANY],
            scratch_shapes=[
                pltpu.VMEM((2, rows + 2 * BLOCK, HEAD_DIM), f32),
                pltpu.VMEM((2, items, 2, BLOCK, HEAD_DIM), b16),
                pltpu.SemaphoreType.DMA((2, items)),
            ],
        ),
        out_shape=(
            jax.ShapeDtypeStruct((rows, width), b16),
            jax.ShapeDtypeStruct((rows, width), b16),
            jax.ShapeDtypeStruct((2, rows, width), f32),
            jax.ShapeDtypeStruct((2, BLOCK, width), b16),
            jax.ShapeDtypeStruct((2, BLOCK, width), b16),
            jax.ShapeDtypeStruct(glob.shape, f32),
            jax.ShapeDtypeStruct(got.shape, b16),
        ),
        compiler_params=pltpu.CompilerParams(vmem_limit_bytes=VMEM_LIMIT),
        name="attend",
    )(place, owner, rank, q, d, k, v, before, after, glob, *([got] * items))


def combine_kernel(capacity, blocks, code, place, hit, own, above, below, glob, got, grad_k, grad_v, acc):
    source = pl.program_id(0)
    rows = blocks * BLOCK

    @pl.when(source == 0)
    def _():
        acc[...] = own[...]

        @pl.when(place[0] > 0)
        def _():
            acc[:, :BLOCK] += below[...].astype(jnp.float32)

        @pl.when(place[1] > 0)
        def _():
            acc[:, rows - BLOCK :] += above[...].astype(jnp.float32)

        for g in range(GLOBALS):

            @pl.when(hit[g] >= 0)
            def _():
                at = pl.ds(pl.multiple_of(hit[g] * BLOCK, BLOCK), BLOCK)
                for head in range(HEADS):
                    column = slice(head * HEAD_DIM, (head + 1) * HEAD_DIM)
                    acc[:, at, column] += glob[head, :, g * BLOCK : (g + 1) * BLOCK].astype(jnp.float32)

    for slot in range(capacity):
        packed = code[source * capacity + slot]

        @pl.when(packed >= 0)
        def _():
            row = pl.ds(pl.multiple_of(packed // HEADS * BLOCK, BLOCK), BLOCK)
            column = pl.ds(pl.multiple_of(packed % HEADS * HEAD_DIM, HEAD_DIM), HEAD_DIM)
            acc[:, row, column] += got[0, slot].astype(jnp.float32)

    @pl.when(source == pl.num_programs(0) - 1)
    def _():
        grad_k[...] = acc[0].astype(jnp.bfloat16)
        grad_v[...] = acc[1].astype(jnp.bfloat16)


def combine(code, place, hit, own, above, below, glob, got):
    shards, capacity = got.shape[:2]
    rows, width = own.shape[1:]

    def whole(a):
        return pl.BlockSpec(a.shape, lambda s, *_: (0,) * a.ndim)

    out = pl.BlockSpec((rows, width), lambda s, *_: (0, 0))
    return pl.pallas_call(
        functools.partial(combine_kernel, capacity, rows // BLOCK),
        grid_spec=pltpu.PrefetchScalarGridSpec(
            num_scalar_prefetch=3,
            grid=(shards,),
            in_specs=[
                whole(own),
                whole(above),
                whole(below),
                whole(glob),
                pl.BlockSpec((1, capacity, 2, BLOCK, HEAD_DIM), lambda s, *_: (s, 0, 0, 0, 0)),
            ],
            out_specs=[out, out],
            scratch_shapes=[pltpu.VMEM((2, rows, width), jnp.float32)],
        ),
        out_shape=(
            jax.ShapeDtypeStruct((rows, width), jnp.bfloat16),
            jax.ShapeDtypeStruct((rows, width), jnp.bfloat16),
        ),
        compiler_params=pltpu.CompilerParams(vmem_limit_bytes=VMEM_LIMIT),
        name="combine",
    )(code, place, hit, own, above, below, glob, got)


def on_device(queries, keys, values, grad_out, global_blocks, random_blocks):
    shards = lax.axis_size("seq")
    me = lax.axis_index("seq")
    blocks = queries.shape[0] // BLOCK
    i32 = jnp.int32

    mine = global_blocks // blocks == me
    parts = []
    for g in range(GLOBALS):
        start = global_blocks[g] % blocks * BLOCK
        pair = jnp.stack(
            [lax.dynamic_slice_in_dim(a, start, BLOCK, 0) for a in (keys, values)], 0
        )
        parts.append(jnp.where(mine[g], pair, jnp.zeros_like(pair)))
    glob = jnp.concatenate(parts, 1).reshape(2, GLOBALS * BLOCK, HEADS, HEAD_DIM)
    glob = jnp.transpose(glob, (2, 0, 1, 3))

    wanted = lax.dynamic_slice_in_dim(random_blocks, me * blocks, blocks, 1).reshape(-1)
    requests = wanted.shape[0]
    capacity = (requests + shards - 1) // shards
    owner = wanted // blocks
    hits = (owner[:, None] == jnp.arange(shards, dtype=i32)[None, :]).astype(i32)
    rank = jnp.sum((jnp.cumsum(hits, 0) - hits) * hits, 1)
    asked = jnp.transpose(random_blocks.reshape(HEADS, shards, blocks, RANDOM), (1, 0, 2, 3))
    asked = asked.reshape(shards, requests)
    served = (asked // blocks == me).astype(i32)
    serve_rank = jnp.cumsum(served, 1) - served
    chosen = served[:, :, None] * (
        serve_rank[:, :, None] == jnp.arange(capacity, dtype=i32)[None, None, :]
    ).astype(i32)
    item_head = jnp.arange(requests, dtype=i32) // (blocks * RANDOM)
    entry = asked % blocks * HEADS + item_head[None, :] + 1
    code = (jnp.sum(chosen * entry[:, :, None], 1) - 1).reshape(-1)

    got, before, after, glob_all = fetch(
        jnp.maximum(code, 0), keys, values, in_quarters(glob, shards), shards, capacity
    )
    glob = glob_all.reshape(glob.shape)
    place = jnp.stack([me, shards - 1 - me]).astype(i32)
    attended, grad_q, own_grad, lower, upper, glob_grad, back = attend(
        place, owner, rank, queries, grad_out, keys, values, before, after, glob, got
    )
    returned, above, below, glob_sum = give_back(
        back, lower, upper, in_quarters(glob_grad.astype(jnp.bfloat16), shards), shards
    )
    glob_sum = glob_sum.reshape(glob.shape)
    hit = jnp.where(mine, global_blocks % blocks, -1).astype(i32)
    grad_k, grad_v = combine(code, place, hit, own_grad, above, below, glob_sum, returned)
    return attended, grad_q, grad_k, grad_v


def solution(mesh):
    rows = P(("groups", "seq"), None)
    return jax.shard_map(
        on_device,
        mesh=mesh,
        in_specs=(rows, rows, rows, rows, P("groups"), P("groups", None, None)),
        out_specs=(rows, rows, rows, rows),
        check_vma=False,
    )
```
